256 devices in a mesh: grp: 16 (over z, x_lo), shard: 16 (over y, x_hi, core).
Axes of the slice: x: 4 (x_hi: 2, x_lo: 2; x = x_hi * 2 + x_lo), y: 4, z: 8, core: 2. Of those that a mesh axis runs over, the one named last changes fastest.
Arguments:
- pooled: bfloat16 [6144, 256, 128], P('grp', 'shard'), may hold values from -6 to 6
- row_scale: float32 [6144, 256], P('grp', 'shard'), may hold values from 0.3 to 3
- row_ids: int32 [6144, 256], P('grp', 'shard'), may hold values from 0 to 255
- feature_order: int32 [256], replicated, may hold values from 0 to 255, each once
- compress_w: bfloat16 [2, 256, 128], replicated, may hold values from -0.375 to 0.375
- expand_w: bfloat16 [2, 128, 128], replicated, may hold values from -0.5 to 0.5
- norm_gain: float32 [2, 128], replicated, may hold values from 0.5 to 1.5
- out_grad: bfloat16 [6144, 256, 128], P(('grp', 'shard')), may hold values from -6 to 6
Outputs:
- features_out: bfloat16 [6144, 256, 128], P(('grp', 'shard'))
- table_grad: float32 [256, 256, 128], P('shard')
- compress_grad: float32 [2, 256, 128], replicated
- expand_grad: float32 [2, 128, 128], replicated
- gain_grad: float32 [2, 128], replicated
The draws below stay inside these ranges and needn't reach their ends.
Inputs may be any that keep to these rules, and one draw needn't show every extreme that they name: `feature_order`: a permutation of 0 .. 255.
All inputs are finite; a program needn't handle non-finite values.
Results may differ from the reference program's by a relative error of at most 0.03.
Values may be sent and summed in bfloat16 or wider, within the bound.
No kernel may reach another device: no remote copies, remote signals or barrier semaphores. Data moves between devices by JAX's collectives and lax.ppermute only.
A program may use at most 128 MiB of HBM per device.

```python
import math
import jax
import jax.numpy as jnp
from jax import lax

F = 256
D = 128
K = 128
L = 2
S_DEV = 24
R = 256
SAMPLES = 6144


def touch_ends(drawn, own_key, low, top_value):
    place = [jax.random.randint(jax.random.fold_in(own_key, axis), (), 0, length) for axis, length in enumerate(drawn.shape)]
    main_axis = drawn.shape.index(max(drawn.shape))
    beside = place[:main_axis] + [(place[main_axis] + 1) % drawn.shape[main_axis]] + place[main_axis + 1:]
    return drawn.at[tuple(place)].set(low).at[tuple(beside)].set(top_value)


def steps_of(key, dims, shards, low, largest):
    gain, own = 1.0, jax.random.fold_in(key, 6)
    for position, shards_of in shards:
        heights = jnp.exp(jax.random.uniform(jax.random.fold_in(own, position), (shards_of,), jnp.float32, low / len(shards), largest / len(shards)))
        gain = gain * jnp.repeat(heights, dims[position] // shards_of).reshape([-1 if axis == position else 1 for axis in range(len(dims))])
    return gain


def noise(key, shape, spread, bound, cuts=(), kind=jnp.bfloat16):
    entries = spread * jax.random.normal(key, shape, jnp.float32)
    if cuts:
        entries = entries * steps_of(key, shape, cuts, -0.22, 0.18)
    return jnp.clip(entries, -bound, bound).astype(kind)


def setup_inputs(seed: int = 0) -> dict:
    keys = jax.random.split(jax.random.key(seed), 9)
    pooled = noise(keys[0], (SAMPLES, F, D), 1.0, 6.0, ((0, 16), (1, 16)))
    row_scale = jnp.clip(jnp.exp(math.log(3.0) - 2.3025851 * jax.random.uniform(keys[1], (SAMPLES, F), jnp.float32) ** steps_of(keys[1], (SAMPLES, F), ((0, 16), (1, 16)), -0.2, 0.2)), 0.3, 3.0)
    row_ids = touch_ends(jax.random.randint(keys[2], (SAMPLES, F), 0, R), jax.random.fold_in(keys[2], 1), 0, R - 1).astype(jnp.int32)
    feature_order = jax.random.permutation(keys[3], F).astype(jnp.int32)
    compress_w = noise(keys[4], (L, F, K), F ** -0.5, 0.375)
    expand_w = noise(keys[5], (L, K, D), K ** -0.5, 0.5)
    norm_gain = jnp.clip(1.0 + 0.1 * jax.random.normal(keys[6], (L, D), jnp.float32), 0.5, 1.5)
    out_grad = noise(keys[7], (SAMPLES, F, D), 1.0, 6.0, ((0, 256),))
    return dict(pooled=pooled, row_scale=row_scale, row_ids=row_ids, feature_order=feature_order, compress_w=compress_w, expand_w=expand_w, norm_gain=norm_gain, out_grad=out_grad)


def layers(x, wcol, expand_w, norm_gain):
    depth = wcol.shape[0]
    width = x.shape[2]
    for layer in range(depth):
        u_mat = jnp.einsum('bfd,fk->bdk', x, wcol[layer], preferred_element_type=jnp.float32).astype(jnp.bfloat16)
        inter = (jnp.einsum('bfd,bdk->bfk', x, u_mat, preferred_element_type=jnp.float32) / jnp.sqrt(jnp.float32(width))).astype(jnp.bfloat16)
        mixed = x.astype(jnp.float32) + jnp.einsum('bfk,kd->bfd', inter, expand_w[layer], preferred_element_type=jnp.float32)
        scale = lax.rsqrt(lax.optimization_barrier(jnp.mean(mixed * mixed, axis=-1, keepdims=True)) + 1e-06)
        x = (mixed * scale * norm_gain[layer]).astype(jnp.bfloat16)
    return x

def reference(pooled, row_scale, row_ids, feature_order, compress_w, expand_w, norm_gain, out_grad):
    wcol = compress_w[:, feature_order, :]
    x_zero = (pooled.astype(jnp.float32) * row_scale[:, :, None]).astype(jnp.bfloat16)
    blocks = SAMPLES // S_DEV

    def one_block(index):
        start = (index * S_DEV).astype(jnp.int32)
        x_block = lax.dynamic_slice_in_dim(x_zero, start, S_DEV, 0)
        c_block = lax.dynamic_slice_in_dim(out_grad, start, S_DEV, 0)
        result, pull = jax.vjp(layers, x_block, wcol, expand_w, norm_gain)
        grad_x0, grad_wcol, grad_expand, grad_gain = pull(c_block)
        return (result, grad_x0, grad_wcol.astype(jnp.float32), grad_expand.astype(jnp.float32), grad_gain.astype(jnp.float32))
    results, grad_x0, grad_wcol, grad_expand, grad_gain = lax.map(one_block, jnp.arange(blocks, dtype=jnp.int32))
    features_out = results.reshape(SAMPLES, F, D)
    grad_x0 = grad_x0.reshape(SAMPLES, F, D)
    wcol_grad = lax.optimization_barrier(jnp.sum(grad_wcol, axis=0))
    compress_grad = jnp.zeros((L, F, K), jnp.float32).at[:, feature_order, :].set(wcol_grad)
    expand_grad = lax.optimization_barrier(jnp.sum(grad_expand, axis=0))
    gain_grad = lax.optimization_barrier(jnp.sum(grad_gain, axis=0))

    def one_table(column):
        values = jnp.take(grad_x0, column, axis=1).astype(jnp.float32) * jnp.take(row_scale, column, axis=1)[:, None]
        return jax.ops.segment_sum(values, jnp.take(row_ids, column, axis=1), num_segments=R)
    table_grad = lax.map(one_table, jnp.arange(F, dtype=jnp.int32))
    return (features_out, table_grad, compress_grad, expand_grad, gain_grad)
```

```python
import jax
import jax.numpy as jnp
from jax import lax
from jax.sharding import Mesh, PartitionSpec as P

R = 256
SHARD = ("y", "xh", "core")
PLANE = ("xl", "y", "xh", "core")


def layers(x, wcol, expand_w, norm_gain):
    depth = wcol.shape[0]
    width = x.shape[2]
    for layer in range(depth):
        u_mat = jnp.einsum(
            "bfd,fk->bdk", x, wcol[layer], preferred_element_type=jnp.float32
        ).astype(jnp.bfloat16)
        inter = (
            jnp.einsum("bfd,bdk->bfk", x, u_mat, preferred_element_type=jnp.float32)
            / jnp.sqrt(jnp.float32(width))
        ).astype(jnp.bfloat16)
        mixed = x.astype(jnp.float32) + jnp.einsum(
            "bfk,kd->bfd", inter, expand_w[layer], preferred_element_type=jnp.float32
        )
        scale = lax.rsqrt(jnp.mean(mixed * mixed, axis=-1, keepdims=True) + 1e-06)
        x = (mixed * scale * norm_gain[layer]).astype(jnp.bfloat16)
    return x


def shift_z(x, step):
    return lax.ppermute(x, "z", [(i, (i + step) % 8) for i in range(8)])


def swap_xl(x):
    return lax.ppermute(x, "xl", [(0, 1), (1, 0)])


def on_device(pooled, row_scale, row_ids, feature_order, compress_w, expand_w, norm_gain, out_grad):
    bf16, f32 = jnp.bfloat16, jnp.float32
    xl = lax.axis_index("xl")
    z = lax.axis_index("z")
    place = (feature_order[None, :] == jnp.arange(256, dtype=jnp.int32)[:, None]).astype(bf16)
    wcol = jnp.einsum("fj,lfk->ljk", place, compress_w, preferred_element_type=f32).astype(bf16)
    scaled = (pooled.astype(f32) * row_scale[:, :, None]).astype(bf16)
    x_zero = lax.all_to_all(scaled, SHARD, split_axis=0, concat_axis=1, tiled=True)

    marks = jnp.stack([row_ids.astype(f32), row_scale]).transpose(0, 2, 1).reshape(2, 2, 8, 384)
    mine = lax.dynamic_index_in_dim(marks, xl, 1, keepdims=False)
    other = swap_xl(lax.dynamic_index_in_dim(marks, 1 - xl, 1, keepdims=False))
    low = xl == 0
    marks = jnp.concatenate([jnp.where(low, mine, other), jnp.where(low, other, mine)], axis=2)

    features_out, pull = jax.vjp(layers, x_zero, wcol, expand_w, norm_gain)
    grad_x, grad_w, grad_v, grad_g = pull(out_grad)
    compress_part = jnp.einsum("fj,ljk->lfk", place, grad_w, preferred_element_type=f32).astype(bf16)
    gain_high = grad_g.astype(bf16)
    gain_low = (grad_g - gain_high.astype(f32)).astype(bf16)
    dense = jnp.concatenate(
        [compress_part.reshape(512, 128), grad_v.reshape(256, 128), gain_high, gain_low, jnp.zeros((252, 128), bf16)]
    )
    parcels = grad_x.reshape(24, 16, 2, 8, 128).transpose(2, 1, 0, 3, 4).reshape(32, 192, 128)
    parcels = jnp.concatenate([parcels, dense.reshape(32, 32, 128)], axis=1)
    parcels = lax.all_to_all(parcels, PLANE, split_axis=0, concat_axis=0, tiled=True)

    dense_part = jnp.sum(parcels[:, 192:].astype(f32), axis=0).astype(bf16)
    grads = parcels[:, :192].reshape(768, 8, 128)
    hit = marks[0][:, None, :] == jnp.arange(R, dtype=f32)[None, :, None]
    scale_high = marks[1].astype(bf16)
    scale_low = (marks[1] - scale_high.astype(f32)).astype(bf16)
    none = jnp.zeros((), bf16)
    high = jnp.einsum("frb,bfd->frd", jnp.where(hit, scale_high[:, None, :], none), grads, preferred_element_type=f32)
    low_part = jnp.einsum("frb,bfd->frd", jnp.where(hit, scale_low[:, None, :], none), grads, preferred_element_type=f32)
    table_part = (high + low_part).astype(bf16)
    table_part = jnp.concatenate([table_part, jnp.broadcast_to(dense_part[None], (8, 32, 128))], axis=1)
    table_part = lax.all_to_all(table_part, "z", split_axis=0, concat_axis=0, tiled=True)
    summed = jnp.sum(table_part.astype(f32), axis=0).astype(bf16)
    table, dense_sum = summed[:256], summed[256:]

    dense_all = lax.all_to_all(
        jnp.broadcast_to(dense_sum[None], (32, 32, 128)), PLANE, split_axis=0, concat_axis=0, tiled=True
    ).reshape(1024, 128).astype(f32)
    compress_grad = dense_all[:512].reshape(2, 256, 128)
    expand_grad = dense_all[512:768].reshape(2, 128, 128)
    gain_grad = dense_all[768:770] + dense_all[770:772]

    other = swap_xl(table)
    pair = jnp.stack([jnp.where(low, table, other), jnp.where(low, other, table)])
    out = jnp.zeros((2, 8, R, 128), f32)

    def put(out, block, owner, start=0):
        return lax.dynamic_update_slice(out, block.astype(f32)[:, None], (0, owner % 8, start, 0))

    out = put(out, pair, z)
    up = down = pair
    for step in range(1, 4):
        up, down = shift_z(up, 1), shift_z(down, -1)
        out = put(out, up, z - step + 8)
        out = put(out, down, z + step)
    half_up = shift_z(up[:, :128], 1)
    half_down = shift_z(down[:, 128:], -1)
    out = put(out, half_up, z + 4)
    out = put(out, half_down, z + 4, 128)
    table_grad = out.reshape(16, R, 128)
    return (features_out, table_grad, compress_grad, expand_grad, gain_grad)


def solution(mesh):
    split = Mesh(mesh.devices.reshape(8, 2, 4, 2, 2), ("z", "xl", "y", "xh", "core"))
    grp = ("z", "xl")
    return jax.shard_map(
        on_device,
        mesh=split,
        in_specs=(
            P(grp, SHARD, None),
            P(grp, SHARD),
            P(grp, SHARD),
            P(),
            P(),
            P(),
            P(),
            P(grp + SHARD, None, None),
        ),
        out_specs=(P(grp + SHARD, None, None), P(SHARD, None, None), P(), P(), P()),
        check_vma=False,
    )
```

```python
import math

import jax
import jax.numpy as jnp
from jax import lax
from jax.experimental import pallas as pl
from jax.experimental.pallas import tpu as pltpu
from jax.sharding import Mesh, PartitionSpec as P

R = 256
SHARD = ("y", "xh", "core")
PLANE = ("xl", "y", "xh", "core")


def dot(a, b, dims=((1,), (0,))):
    return lax.dot_general(a, b, (dims, ((), ())), preferred_element_type=jnp.float32)


NT = ((1,), (1,))
TN = ((0,), (0,))
B = 4


def layers_kernel(x_ref, og_ref, w_ref, wt_ref, v_ref, gain_ref, place_ref, feat_ref, out_ref, dw, dv, dg):
    step = pl.program_id(0)
    bf16, f32 = jnp.bfloat16, jnp.float32
    root = 1.0 / math.sqrt(128.0)

    @pl.when(step == 0)
    def _():
        dw[...] = jnp.zeros_like(dw)
        dv[...] = jnp.zeros_like(dv)
        dg[...] = jnp.zeros_like(dg)

    x = [x_ref[:, b].reshape(256, 128) for b in range(B)]
    saved = []
    for layer in range(2):
        gain = gain_ref[layer : layer + 1, :]
        ut = [dot(wt_ref[layer], x[b]).astype(bf16) for b in range(B)]
        inter = [(dot(x[b], ut[b], NT) * root).astype(bf16) for b in range(B)]
        kept = []
        after = []
        for b in range(B):
            z = x[b].astype(f32) + dot(inter[b], v_ref[layer])
            r = lax.rsqrt(jnp.mean(z * z, axis=-1, keepdims=True) + 1e-06)
            n = z * r
            kept.append((n, r))
            after.append((n * gain).astype(bf16))
        saved.append((x, ut, inter, kept))
        x = after
    for b in range(B):
        feat_ref[b] = x[b]
    c = [og_ref[b].astype(f32) for b in range(B)]
    for layer in (1, 0):
        gain = gain_ref[layer : layer + 1, :]
        x, ut, inter, kept = saved[layer]
        below = []
        dw_sum = 0.0
        dv_sum = 0.0
        dg_sum = 0.0
        for b in range(B):
            n, r = kept[b]
            cn = c[b] * n
            dg_sum = dg_sum + jnp.sum(cn.reshape(32, 8, 128), axis=0)
            mean = jnp.mean(cn * gain, axis=-1, keepdims=True)
            dz = r * (c[b] * gain - n * mean)
            dzb = dz.astype(bf16)
            dv_sum = dv_sum + dot(inter[b], dzb, TN)
            dint = dot(dzb, v_ref[layer], NT).astype(bf16)
            dut = dot(dint, x[b], TN).astype(bf16)
            left = jnp.concatenate([dint, w_ref[layer]], axis=1)
            right = jnp.concatenate([ut[b], dut], axis=0)
            dx = (dz + dot(left, right) * root).astype(bf16)
            dw_sum = dw_sum + dot(x[b], dut, NT)
            below.append(dx.astype(f32))
        dw[layer] += dw_sum
        dv[layer] += dv_sum
        dg[layer] += dg_sum
        c = below
    for b in range(0, B, 2):
        first = c[b].reshape(16, 2, 8, 128)
        second = c[b + 1].reshape(16, 2, 8, 128)
        rows = pl.ds(pl.multiple_of(step * (B * 8) + b * 8, 16), 16)
        for half in range(2):
            both = jnp.concatenate([first[:, half], second[:, half]], axis=1)
            out_ref[half * 16 : half * 16 + 16, rows, :] = both.astype(bf16)

    @pl.when(step == pl.num_programs(0) - 1)
    def _():
        for layer in range(2):
            grad = (dw[layer] * root).astype(bf16)
            moved = dot(place_ref[...], grad).astype(bf16)
            out_ref[layer * 8 : layer * 8 + 8, 192:224, :] = moved.reshape(8, 32, 128)
            out_ref[16 + layer * 4 : 20 + layer * 4, 192:224, :] = dv[layer].astype(bf16).reshape(4, 32, 128)
        total = jnp.sum(dg[...], axis=1)
        high = total.astype(bf16).astype(f32)
        rest = jnp.concatenate([high, total - high, jnp.zeros((28, 128), f32)], axis=0)
        out_ref[24, 192:224, :] = rest.astype(bf16)
        out_ref[25:32, 192:224, :] = jnp.zeros((7, 32, 128), bf16)


def run_layers(x, out_grad, wcol, wcol_t, expand_w, norm_gain, place):
    bf16, f32 = jnp.bfloat16, jnp.float32
    whole = lambda *shape: pl.BlockSpec(shape, lambda i: (0,) * len(shape))
    return pl.pallas_call(
        layers_kernel,
        grid=(24 // B,),
        out_shape=(
            jax.ShapeDtypeStruct((24, 256, 128), bf16),
            jax.ShapeDtypeStruct((32, 224, 128), bf16),
        ),
        in_specs=[
            pl.BlockSpec((16, B, 16, 128), lambda i: (0, i, 0, 0)),
            pl.BlockSpec((B, 256, 128), lambda i: (i, 0, 0)),
            whole(2, 256, 128),
            whole(2, 128, 256),
            whole(2, 128, 128),
            whole(2, 128),
            whole(256, 256),
        ],
        out_specs=(pl.BlockSpec((B, 256, 128), lambda i: (i, 0, 0)), whole(32, 224, 128)),
        scratch_shapes=[
            pltpu.VMEM((2, 256, 128), f32),
            pltpu.VMEM((2, 128, 128), f32),
            pltpu.VMEM((2, 8, 128), f32),
        ],
        compiler_params=pltpu.CompilerParams(vmem_limit_bytes=40 * 1024 * 1024),
        cost_estimate=pl.CostEstimate(flops=4 * 10**9, bytes_accessed=7 * 2**20, transcendentals=0),
        name="layers",
    )(x, out_grad, wcol, wcol_t, expand_w, norm_gain, place)


def shift_z(x, step):
    return lax.ppermute(x, "z", [(i, (i + step) % 8) for i in range(8)])


def swap_xl(x):
    return lax.ppermute(x, "xl", [(0, 1), (1, 0)])


def on_device(pooled, row_scale, row_ids, feature_order, compress_w, expand_w, norm_gain, out_grad):
    bf16, f32 = jnp.bfloat16, jnp.float32
    xl = lax.axis_index("xl")
    z = lax.axis_index("z")
    place = (feature_order[None, :] == jnp.arange(256, dtype=jnp.int32)[:, None]).astype(bf16)
    wcol = jnp.einsum("fj,lfk->ljk", place, compress_w, preferred_element_type=f32).astype(bf16)
    scaled = (pooled.astype(f32) * row_scale[:, :, None]).astype(bf16)
    wcol_t = jnp.einsum("fj,lfk->lkj", place, compress_w, preferred_element_type=f32).astype(bf16)
    x_zero = lax.all_to_all(scaled, SHARD, split_axis=0, concat_axis=0, tiled=True).reshape(16, 24, 16, 128)

    marks = jnp.stack([row_ids.astype(f32), row_scale]).transpose(0, 2, 1).reshape(2, 2, 8, 384)
    mine = lax.dynamic_index_in_dim(marks, xl, 1, keepdims=False)
    other = swap_xl(lax.dynamic_index_in_dim(marks, 1 - xl, 1, keepdims=False))
    low = xl == 0
    marks = jnp.concatenate([jnp.where(low, mine, other), jnp.where(low, other, mine)], axis=2)

    features_out, parcels = run_layers(x_zero, out_grad, wcol, wcol_t, expand_w, norm_gain, place)
    parcels = lax.all_to_all(parcels, PLANE, split_axis=0, concat_axis=0, tiled=True)

    dense_part = jnp.sum(parcels[:, 192:].astype(f32), axis=0).astype(bf16)
    grads = parcels[:, :192].reshape(768, 8, 128)
    hit = marks[0][:, None, :] == jnp.arange(R, dtype=f32)[None, :, None]
    scale_high = marks[1].astype(bf16)
    scale_low = (marks[1] - scale_high.astype(f32)).astype(bf16)
    none = jnp.zeros((), bf16)
    high = jnp.einsum("frb,bfd->frd", jnp.where(hit, scale_high[:, None, :], none), grads, preferred_element_type=f32)
    low_part = jnp.einsum("frb,bfd->frd", jnp.where(hit, scale_low[:, None, :], none), grads, preferred_element_type=f32)
    table_part = (high + low_part).astype(bf16)
    table_part = jnp.concatenate([table_part, jnp.broadcast_to(dense_part[None], (8, 32, 128))], axis=1)
    table_part = lax.all_to_all(table_part, "z", split_axis=0, concat_axis=0, tiled=True)
    summed = jnp.sum(table_part.astype(f32), axis=0).astype(bf16)
    table, dense_sum = summed[:256], summed[256:]

    dense_all = lax.all_to_all(
        jnp.broadcast_to(dense_sum[None], (32, 32, 128)), PLANE, split_axis=0, concat_axis=0, tiled=True
    ).reshape(1024, 128).astype(f32)
    compress_grad = dense_all[:512].reshape(2, 256, 128)
    expand_grad = dense_all[512:768].reshape(2, 128, 128)
    gain_grad = dense_all[768:770] + dense_all[770:772]

    other = swap_xl(table)
    pair = jnp.stack([jnp.where(low, table, other), jnp.where(low, other, table)])
    out = jnp.zeros((2, 8, R, 128), f32)

    def put(out, block, owner, start=0):
        return lax.dynamic_update_slice(out, block.astype(f32)[:, None], (0, owner % 8, start, 0))

    out = put(out, pair, z)
    up = down = pair
    for step in range(1, 4):
        up, down = shift_z(up, 1), shift_z(down, -1)
        out = put(out, up, z - step + 8)
        out = put(out, down, z + step)
    half_up = shift_z(up[:, :128], 1)
    half_down = shift_z(down[:, 128:], -1)
    out = put(out, half_up, z + 4)
    out = put(out, half_down, z + 4, 128)
    table_grad = out.reshape(16, R, 128)
    return (features_out, table_grad, compress_grad, expand_grad, gain_grad)


def solution(mesh):
    split = Mesh(mesh.devices.reshape(8, 2, 4, 2, 2), ("z", "xl", "y", "xh", "core"))
    grp = ("z", "xl")
    return jax.shard_map(
        on_device,
        mesh=split,
        in_specs=(
            P(grp, SHARD, None),
            P(grp, SHARD),
            P(grp, SHARD),
            P(),
            P(),
            P(),
            P(),
            P(grp + SHARD, None, None),
        ),
        out_specs=(P(grp + SHARD, None, None), P(SHARD, None, None), P(), P(), P()),
        check_vma=False,
    )
```

```python
import math

import jax
import jax.numpy as jnp
from jax import lax
from jax.experimental import pallas as pl
from jax.experimental.pallas import tpu as pltpu
from jax.sharding import Mesh, PartitionSpec as P

R = 256
SHARD = ("y", "xh", "core")
PLANE = ("xl", "y", "xh", "core")


def dot(a, b, dims=((1,), (0,))):
    return lax.dot_general(a, b, (dims, ((), ())), preferred_element_type=jnp.float32)


NT = ((1,), (1,))
TN = ((0,), (0,))
B = 12
G = 6


def layers_kernel(x_ref, og_ref, w_ref, wt_ref, v_ref, gain_ref, place_ref, feat_ref, out_ref, dw, dv, dg):
    step = pl.program_id(0)
    bf16, f32 = jnp.bfloat16, jnp.float32
    root = 1.0 / math.sqrt(128.0)

    @pl.when(step == 0)
    def _():
        dw[...] = jnp.zeros_like(dw)
        dv[...] = jnp.zeros_like(dv)
        dg[...] = jnp.zeros_like(dg)

    x = [x_ref[:, b].reshape(256, 128) for b in range(B)]
    saved = []
    for layer in range(2):
        gain = gain_ref[layer : layer + 1, :]
        ut = [dot(wt_ref[layer], x[b]).astype(bf16) for b in range(B)]
        inter = [(dot(x[b], ut[b], NT) * root).astype(bf16) for b in range(B)]
        kept = []
        after = []
        for b in range(B):
            z = x[b].astype(f32) + dot(inter[b], v_ref[layer])
            r = lax.rsqrt(jnp.mean(z * z, axis=-1, keepdims=True) + 1e-06)
            n = z * r
            kept.append((n, r))
            after.append((n * gain).astype(bf16))
        saved.append((x, ut, inter, kept))
        x = after
    for b in range(B):
        feat_ref[b] = x[b]
    c = [og_ref[b].astype(f32) for b in range(B)]
    for layer in (1, 0):
        gain = gain_ref[layer : layer + 1, :]
        x, ut, inter, kept = saved[layer]
        below = []
        dw_sum = 0.0
        dv_sum = 0.0
        dg_sum = 0.0
        for start in range(0, B, G):
            group = range(start, start + G)
            dz, dzb, dint, dut = {}, {}, {}, {}
            for b in group:
                n, r = kept[b]
                cn = c[b] * n
                dg_sum = dg_sum + jnp.sum(cn.reshape(32, 8, 128), axis=0)
                mean = jnp.mean(cn * gain, axis=-1, keepdims=True)
                dz[b] = r * (c[b] * gain - n * mean)
                dzb[b] = dz[b].astype(bf16)
            for b in group:
                dint[b] = dot(dzb[b], v_ref[layer], NT).astype(bf16)
            for b in group:
                dv_sum = dv_sum + dot(inter[b], dzb[b], TN)
            for b in group:
                dut[b] = dot(dint[b], x[b], TN).astype(bf16)
            for b in group:
                left = jnp.concatenate([dint[b], w_ref[layer]], axis=1)
                right = jnp.concatenate([ut[b], dut[b]], axis=0)
                below.append((dz[b] + dot(left, right) * root).astype(bf16).astype(f32))
            for b in group:
                dw_sum = dw_sum + dot(x[b], dut[b], NT)
        dw[layer] += dw_sum
        dv[layer] += dv_sum
        dg[layer] += dg_sum
        c = below
    for b in range(0, B, 2):
        first = c[b].reshape(16, 2, 8, 128)
        second = c[b + 1].reshape(16, 2, 8, 128)
        rows = pl.ds(pl.multiple_of(step * (B * 8) + b * 8, 16), 16)
        for half in range(2):
            both = jnp.concatenate([first[:, half], second[:, half]], axis=1)
            out_ref[half * 16 : half * 16 + 16, rows, :] = both.astype(bf16)

    @pl.when(step == pl.num_programs(0) - 1)
    def _():
        for layer in range(2):
            grad = (dw[layer] * root).astype(bf16)
            moved = dot(place_ref[...], grad).astype(bf16)
            out_ref[layer * 8 : layer * 8 + 8, 192:224, :] = moved.reshape(8, 32, 128)
            out_ref[16 + layer * 4 : 20 + layer * 4, 192:224, :] = dv[layer].astype(bf16).reshape(4, 32, 128)
        total = jnp.sum(dg[...], axis=1)
        high = total.astype(bf16).astype(f32)
        rest = jnp.concatenate([high, total - high, jnp.zeros((28, 128), f32)], axis=0)
        out_ref[24, 192:224, :] = rest.astype(bf16)
        out_ref[25:32, 192:224, :] = jnp.zeros((7, 32, 128), bf16)


def run_layers(x, out_grad, wcol, wcol_t, expand_w, norm_gain, place):
    bf16, f32 = jnp.bfloat16, jnp.float32
    whole = lambda *shape: pl.BlockSpec(shape, lambda i: (0,) * len(shape))
    return pl.pallas_call(
        layers_kernel,
        grid=(24 // B,),
        out_shape=(
            jax.ShapeDtypeStruct((24, 256, 128), bf16),
            jax.ShapeDtypeStruct((32, 224, 128), bf16),
        ),
        in_specs=[
            pl.BlockSpec((16, B, 16, 128), lambda i: (0, i, 0, 0)),
            pl.BlockSpec((B, 256, 128), lambda i: (i, 0, 0)),
            whole(2, 256, 128),
            whole(2, 128, 256),
            whole(2, 128, 128),
            whole(2, 128),
            whole(256, 256),
        ],
        out_specs=(pl.BlockSpec((B, 256, 128), lambda i: (i, 0, 0)), whole(32, 224, 128)),
        scratch_shapes=[
            pltpu.VMEM((2, 256, 128), f32),
            pltpu.VMEM((2, 128, 128), f32),
            pltpu.VMEM((2, 8, 128), f32),
        ],
        compiler_params=pltpu.CompilerParams(vmem_limit_bytes=40 * 1024 * 1024),
        cost_estimate=pl.CostEstimate(flops=4 * 10**9, bytes_accessed=7 * 2**20, transcendentals=0),
        name="layers",
    )(x, out_grad, wcol, wcol_t, expand_w, norm_gain, place)


def shift_z(x, step):
    return lax.ppermute(x, "z", [(i, (i + step) % 8) for i in range(8)])


def swap_xl(x):
    return lax.ppermute(x, "xl", [(0, 1), (1, 0)])


def on_device(pooled, row_scale, row_ids, feature_order, compress_w, expand_w, norm_gain, out_grad):
    bf16, f32 = jnp.bfloat16, jnp.float32
    xl = lax.axis_index("xl")
    z = lax.axis_index("z")
    place = (feature_order[None, :] == jnp.arange(256, dtype=jnp.int32)[:, None]).astype(bf16)
    wcol = jnp.einsum("fj,lfk->ljk", place, compress_w, preferred_element_type=f32).astype(bf16)
    scaled = (pooled.astype(f32) * row_scale[:, :, None]).astype(bf16)
    wcol_t = jnp.einsum("fj,lfk->lkj", place, compress_w, preferred_element_type=f32).astype(bf16)
    x_zero = lax.all_to_all(scaled, SHARD, split_axis=0, concat_axis=0, tiled=True).reshape(16, 24, 16, 128)

    marks = jnp.stack([row_ids.astype(f32), row_scale]).transpose(0, 2, 1).reshape(2, 2, 8, 384)
    mine = lax.dynamic_index_in_dim(marks, xl, 1, keepdims=False)
    other = swap_xl(lax.dynamic_index_in_dim(marks, 1 - xl, 1, keepdims=False))
    low = xl == 0
    marks = jnp.concatenate([jnp.where(low, mine, other), jnp.where(low, other, mine)], axis=2)

    features_out, parcels = run_layers(x_zero, out_grad, wcol, wcol_t, expand_w, norm_gain, place)
    parcels = lax.all_to_all(parcels, PLANE, split_axis=0, concat_axis=0, tiled=True)

    dense_part = jnp.sum(parcels[:, 192:].astype(f32), axis=0).astype(bf16)
    grads = parcels[:, :192].reshape(768, 8, 128)
    hit = marks[0][:, None, :] == jnp.arange(R, dtype=f32)[None, :, None]
    scale_high = marks[1].astype(bf16)
    scale_low = (marks[1] - scale_high.astype(f32)).astype(bf16)
    none = jnp.zeros((), bf16)
    high = jnp.einsum("frb,bfd->frd", jnp.where(hit, scale_high[:, None, :], none), grads, preferred_element_type=f32)
    low_part = jnp.einsum("frb,bfd->frd", jnp.where(hit, scale_low[:, None, :], none), grads, preferred_element_type=f32)
    table_part = (high + low_part).astype(bf16)
    table_part = jnp.concatenate([table_part, jnp.broadcast_to(dense_part[None], (8, 32, 128))], axis=1)
    table_part = lax.all_to_all(table_part, "z", split_axis=0, concat_axis=0, tiled=True)
    summed = jnp.sum(table_part.astype(f32), axis=0).astype(bf16)
    table, dense_sum = summed[:256], summed[256:]

    dense_all = lax.all_to_all(
        jnp.broadcast_to(dense_sum[None], (32, 32, 128)), PLANE, split_axis=0, concat_axis=0, tiled=True
    ).reshape(1024, 128).astype(f32)
    compress_grad = dense_all[:512].reshape(2, 256, 128)
    expand_grad = dense_all[512:768].reshape(2, 128, 128)
    gain_grad = dense_all[768:770] + dense_all[770:772]

    other = swap_xl(table)
    pair = jnp.stack([jnp.where(low, table, other), jnp.where(low, other, table)])
    out = jnp.zeros((2, 8, R, 128), f32)

    def put(out, block, owner, start=0):
        return lax.dynamic_update_slice(out, block.astype(f32)[:, None], (0, owner % 8, start, 0))

    out = put(out, pair, z)
    up = down = pair
    for step in range(1, 4):
        up, down = shift_z(up, 1), shift_z(down, -1)
        out = put(out, up, z - step + 8)
        out = put(out, down, z + step)
    half_up = shift_z(up[:, :128], 1)
    half_down = shift_z(down[:, 128:], -1)
    out = put(out, half_up, z + 4)
    out = put(out, half_down, z + 4, 128)
    table_grad = out.reshape(16, R, 128)
    return (features_out, table_grad, compress_grad, expand_grad, gain_grad)


def solution(mesh):
    split = Mesh(mesh.devices.reshape(8, 2, 4, 2, 2), ("z", "xl", "y", "xh", "core"))
    grp = ("z", "xl")
    return jax.shard_map(
        on_device,
        mesh=split,
        in_specs=(
            P(grp, SHARD, None),
            P(grp, SHARD),
            P(grp, SHARD),
            P(),
            P(),
            P(),
            P(),
            P(grp + SHARD, None, None),
        ),
        out_specs=(P(grp + SHARD, None, None), P(SHARD, None, None), P(), P(), P()),
        check_vma=False,
    )
```

```python
import math

import jax
import jax.numpy as jnp
from jax import lax
from jax.experimental import pallas as pl
from jax.experimental.pallas import tpu as pltpu
from jax.sharding import Mesh, PartitionSpec as P

R = 256
SHARD = ("y", "xh", "core")
PLANE = ("xl", "y", "xh", "core")


def dot(a, b, dims=((1,), (0,))):
    return lax.dot_general(a, b, (dims, ((), ())), preferred_element_type=jnp.float32)


NT = ((1,), (1,))
TN = ((0,), (0,))
B = 12
G = 6


def layers_kernel(x_ref, og_ref, w_ref, wt_ref, v_ref, gain_ref, place_ref, feat_ref, out_ref, dw, dv, dg):
    step = pl.program_id(0)
    bf16, f32 = jnp.bfloat16, jnp.float32
    root = 1.0 / math.sqrt(128.0)

    @pl.when(step == 0)
    def _():
        dw[...] = jnp.zeros_like(dw)
        dv[...] = jnp.zeros_like(dv)
        dg[...] = jnp.zeros_like(dg)

    x = [x_ref[:, b].reshape(256, 128) for b in range(B)]
    saved = []
    for layer in range(2):
        gain = gain_ref[layer : layer + 1, :]
        ut = [dot(wt_ref[layer], x[b]).astype(bf16) for b in range(B)]
        inter = [(dot(x[b], ut[b], NT) * root).astype(bf16) for b in range(B)]
        kept = []
        after = []
        for b in range(B):
            z = x[b].astype(f32) + dot(inter[b], v_ref[layer])
            r = lax.rsqrt(jnp.mean(z * z, axis=-1, keepdims=True) + 1e-06)
            n = z * r
            kept.append((n, r))
            after.append((n * gain).astype(bf16))
        saved.append((x, ut, inter, kept))
        x = after
    for b in range(B):
        feat_ref[b] = x[b]
    c = [og_ref[b].astype(f32) for b in range(B)]
    for layer in (1, 0):
        gain = gain_ref[layer : layer + 1, :]
        x, ut, inter, kept = saved[layer]
        below = []
        dw_sum = 0.0
        dv_sum = 0.0
        dg_sum = 0.0
        for start in range(0, B, G):
            group = range(start, start + G)
            dz, dzb, dint, dut = {}, {}, {}, {}
            for b in group:
                n, r = kept[b]
                cn = c[b] * n
                dg_sum = dg_sum + jnp.sum(cn.reshape(32, 8, 128), axis=0)
                mean = jnp.mean(cn * gain, axis=-1, keepdims=True)
                dz[b] = r * (c[b] * gain - n * mean)
                dzb[b] = dz[b].astype(bf16)
            for b in group:
                dint[b] = dot(dzb[b], v_ref[layer], NT).astype(bf16)
            for b in group:
                dv_sum = dv_sum + dot(inter[b], dzb[b], TN)
            for b in group:
                dut[b] = dot(dint[b], x[b], TN).astype(bf16)
            for b in group:
                left = jnp.concatenate([dint[b], w_ref[layer]], axis=1)
                right = jnp.concatenate([ut[b], dut[b]], axis=0)
                below.append((dz[b] + dot(left, right) * root).astype(bf16).astype(f32))
            for b in group:
                dw_sum = dw_sum + dot(x[b], dut[b], NT)
        dw[layer] += dw_sum
        dv[layer] += dv_sum
        dg[layer] += dg_sum
        c = below
    for b in range(0, B, 2):
        first = c[b].reshape(16, 2, 8, 128)
        second = c[b + 1].reshape(16, 2, 8, 128)
        rows = pl.ds(pl.multiple_of(step * (B * 8) + b * 8, 16), 16)
        for half in range(2):
            both = jnp.concatenate([first[:, half], second[:, half]], axis=1)
            out_ref[half * 16 : half * 16 + 16, rows, :] = both.astype(bf16)

    @pl.when(step == pl.num_programs(0) - 1)
    def _():
        for layer in range(2):
            grad = (dw[layer] * root).astype(bf16)
            moved = dot(place_ref[...], grad).astype(bf16)
            out_ref[layer * 8 : layer * 8 + 8, 192:224, :] = moved.reshape(8, 32, 128)
            out_ref[16 + layer * 4 : 20 + layer * 4, 192:224, :] = dv[layer].astype(bf16).reshape(4, 32, 128)
        total = jnp.sum(dg[...], axis=1)
        high = total.astype(bf16).astype(f32)
        rest = jnp.concatenate([high, total - high, jnp.zeros((28, 128), f32)], axis=0)
        out_ref[24, 192:224, :] = rest.astype(bf16)
        out_ref[25:32, 192:224, :] = jnp.zeros((7, 32, 128), bf16)


def run_layers(x, out_grad, wcol, wcol_t, expand_w, norm_gain, place):
    bf16, f32 = jnp.bfloat16, jnp.float32
    whole = lambda *shape: pl.BlockSpec(shape, lambda i: (0,) * len(shape))
    return pl.pallas_call(
        layers_kernel,
        grid=(24 // B,),
        out_shape=(
            jax.ShapeDtypeStruct((24, 256, 128), bf16),
            jax.ShapeDtypeStruct((32, 224, 128), bf16),
        ),
        in_specs=[
            pl.BlockSpec((16, B, 16, 128), lambda i: (0, i, 0, 0)),
            pl.BlockSpec((B, 256, 128), lambda i: (i, 0, 0)),
            whole(2, 256, 128),
            whole(2, 128, 256),
            whole(2, 128, 128),
            whole(2, 128),
            whole(256, 256),
        ],
        out_specs=(pl.BlockSpec((B, 256, 128), lambda i: (i, 0, 0)), whole(32, 224, 128)),
        scratch_shapes=[
            pltpu.VMEM((2, 256, 128), f32),
            pltpu.VMEM((2, 128, 128), f32),
            pltpu.VMEM((2, 8, 128), f32),
        ],
        compiler_params=pltpu.CompilerParams(vmem_limit_bytes=40 * 1024 * 1024),
        cost_estimate=pl.CostEstimate(flops=4 * 10**9, bytes_accessed=7 * 2**20, transcendentals=0),
        name="layers",
    )(x, out_grad, wcol, wcol_t, expand_w, norm_gain, place)


def shift_z(x, step):
    return lax.ppermute(x, "z", [(i, (i + step) % 8) for i in range(8)])


def swap_xl(x):
    return lax.ppermute(x, "xl", [(0, 1), (1, 0)])


def on_device(pooled, row_scale, row_ids, feature_order, compress_w, expand_w, norm_gain, out_grad):
    bf16, f32 = jnp.bfloat16, jnp.float32
    xl = lax.axis_index("xl")
    z = lax.axis_index("z")
    place = (feature_order[None, :] == jnp.arange(256, dtype=jnp.int32)[:, None]).astype(bf16)
    wcol = jnp.einsum("fj,lfk->ljk", place, compress_w, preferred_element_type=f32).astype(bf16)
    scaled = (pooled.astype(f32) * row_scale[:, :, None]).astype(bf16)
    wcol_t = jnp.einsum("fj,lfk->lkj", place, compress_w, preferred_element_type=f32).astype(bf16)
    x_zero = lax.all_to_all(scaled, SHARD, split_axis=0, concat_axis=0, tiled=True).reshape(16, 24, 16, 128)

    marks = jnp.stack([row_ids.astype(f32), row_scale]).transpose(0, 2, 1).reshape(2, 2, 8, 384)
    mine = lax.dynamic_index_in_dim(marks, xl, 1, keepdims=False)
    other = swap_xl(lax.dynamic_index_in_dim(marks, 1 - xl, 1, keepdims=False))
    low = xl == 0
    marks = jnp.concatenate([jnp.where(low, mine, other), jnp.where(low, other, mine)], axis=2)

    features_out, parcels = run_layers(x_zero, out_grad, wcol, wcol_t, expand_w, norm_gain, place)
    parcels = lax.all_to_all(parcels, PLANE, split_axis=0, concat_axis=0, tiled=True)

    dense_part = jnp.sum(parcels[:, 192:].astype(f32), axis=0).astype(bf16)
    grads = parcels[:, :192].reshape(768, 8, 128)
    hit = marks[0][:, None, :] == jnp.arange(R, dtype=f32)[None, :, None]
    scale_high = marks[1].astype(bf16)
    scale_low = (marks[1] - scale_high.astype(f32)).astype(bf16)
    none = jnp.zeros((), bf16)
    high = jnp.einsum("frb,bfd->frd", jnp.where(hit, scale_high[:, None, :], none), grads, preferred_element_type=f32)
    low_part = jnp.einsum("frb,bfd->frd", jnp.where(hit, scale_low[:, None, :], none), grads, preferred_element_type=f32)
    table_part = (high + low_part).astype(bf16)
    table_part = jnp.concatenate([table_part, jnp.broadcast_to(dense_part[None], (8, 32, 128))], axis=1)
    table_part = lax.all_to_all(table_part, "z", split_axis=0, concat_axis=0, tiled=True)
    summed = jnp.sum(table_part.astype(f32), axis=0).astype(bf16)
    table, dense_sum = summed[:256], summed[256:]

    dense_all = lax.all_to_all(
        jnp.broadcast_to(dense_sum[None], (32, 32, 128)), PLANE, split_axis=0, concat_axis=0, tiled=True
    ).reshape(1024, 128)
    other = swap_xl(table)
    pair = jnp.stack([jnp.where(low, table, other), jnp.where(low, other, table)])
    out = jnp.zeros((2, 8, R, 128), f32)

    def put(out, block, owner, start=0):
        return lax.dynamic_update_slice(out, block.astype(f32)[:, None], (0, owner % 8, start, 0))

    out = put(out, pair, z)
    up = down = pair
    for step in range(1, 4):
        up, down = shift_z(up, 1), shift_z(down, -1)
        out = put(out, up, z - step + 8)
        out = put(out, down, z + step)
    up, down, dense_all = lax.optimization_barrier((up, down, dense_all))
    half_up = shift_z(up[:, :128], 1)
    half_down = shift_z(down[:, 128:], -1)
    out = put(out, half_up, z + 4)
    out = put(out, half_down, z + 4, 128)
    table_grad = out.reshape(16, R, 128)
    dense_all = dense_all.astype(f32)
    compress_grad = dense_all[:512].reshape(2, 256, 128)
    expand_grad = dense_all[512:768].reshape(2, 128, 128)
    gain_grad = dense_all[768:770] + dense_all[770:772]

    return (features_out, table_grad, compress_grad, expand_grad, gain_grad)


def solution(mesh):
    split = Mesh(mesh.devices.reshape(8, 2, 4, 2, 2), ("z", "xl", "y", "xh", "core"))
    grp = ("z", "xl")
    return jax.shard_map(
        on_device,
        mesh=split,
        in_specs=(
            P(grp, SHARD, None),
            P(grp, SHARD),
            P(grp, SHARD),
            P(),
            P(),
            P(),
            P(),
            P(grp + SHARD, None, None),
        ),
        out_specs=(P(grp + SHARD, None, None), P(SHARD, None, None), P(), P(), P()),
        check_vma=False,
    )
```

```python
import math

import jax
import jax.numpy as jnp
from jax import lax
from jax.experimental import pallas as pl
from jax.experimental.pallas import tpu as pltpu
from jax.sharding import Mesh, PartitionSpec as P

R = 256
SHARD = ("y", "xh", "core")
PLANE = ("xl", "y", "xh", "core")


def dot(a, b, dims=((1,), (0,))):
    return lax.dot_general(a, b, (dims, ((), ())), preferred_element_type=jnp.float32)


NT = ((1,), (1,))
TN = ((0,), (0,))
B = 24
G = 6


def layers_kernel(x_ref, og_ref, w_ref, wt_ref, v_ref, gain_ref, place_ref, feat_ref, out_ref, dw, dv, dg):
    step = pl.program_id(0)
    bf16, f32 = jnp.bfloat16, jnp.float32
    root = 1.0 / math.sqrt(128.0)

    @pl.when(step == 0)
    def _():
        dw[...] = jnp.zeros_like(dw)
        dv[...] = jnp.zeros_like(dv)
        dg[...] = jnp.zeros_like(dg)

    x = [x_ref[:, b].reshape(256, 128) for b in range(B)]
    saved = []
    for layer in range(2):
        gain = gain_ref[layer : layer + 1, :]
        ut = [dot(wt_ref[layer], x[b]).astype(bf16) for b in range(B)]
        inter = [(dot(x[b], ut[b], NT) * root).astype(bf16) for b in range(B)]
        kept = []
        after = []
        for b in range(B):
            z = x[b].astype(f32) + dot(inter[b], v_ref[layer])
            r = lax.rsqrt(jnp.mean(z * z, axis=-1, keepdims=True) + 1e-06)
            n = z * r
            kept.append((n, r))
            after.append((n * gain).astype(bf16))
        saved.append((x, ut, inter, kept))
        x = after
    for b in range(B):
        feat_ref[b] = x[b]
    c = [og_ref[b].astype(f32) for b in range(B)]
    for layer in (1, 0):
        gain = gain_ref[layer : layer + 1, :]
        x, ut, inter, kept = saved[layer]
        below = []
        dw_sum = 0.0
        dv_sum = 0.0
        dg_sum = 0.0
        for start in range(0, B, G):
            group = range(start, start + G)
            dz, dzb, dint, dut = {}, {}, {}, {}
            for b in group:
                n, r = kept[b]
                cn = c[b] * n
                dg_sum = dg_sum + jnp.sum(cn.reshape(32, 8, 128), axis=0)
                mean = jnp.mean(cn * gain, axis=-1, keepdims=True)
                dz[b] = r * (c[b] * gain - n * mean)
                dzb[b] = dz[b].astype(bf16)
            for b in group:
                dint[b] = dot(dzb[b], v_ref[layer], NT).astype(bf16)
            for b in group:
                dv_sum = dv_sum + dot(inter[b], dzb[b], TN)
            for b in group:
                dut[b] = dot(dint[b], x[b], TN).astype(bf16)
            for b in group:
                left = jnp.concatenate([dint[b], w_ref[layer]], axis=1)
                right = jnp.concatenate([ut[b], dut[b]], axis=0)
                below.append((dz[b] + dot(left, right) * root).astype(bf16).astype(f32))
            for b in group:
                dw_sum = dw_sum + dot(x[b], dut[b], NT)
        dw[layer] += dw_sum
        dv[layer] += dv_sum
        dg[layer] += dg_sum
        c = below
    for b in range(0, B, 2):
        first = c[b].reshape(16, 2, 8, 128)
        second = c[b + 1].reshape(16, 2, 8, 128)
        rows = pl.ds(pl.multiple_of(step * (B * 8) + b * 8, 16), 16)
        for half in range(2):
            both = jnp.concatenate([first[:, half], second[:, half]], axis=1)
            out_ref[half * 16 : half * 16 + 16, rows, :] = both.astype(bf16)

    @pl.when(step == pl.num_programs(0) - 1)
    def _():
        for layer in range(2):
            grad = (dw[layer] * root).astype(bf16)
            moved = dot(place_ref[...], grad).astype(bf16)
            out_ref[layer * 8 : layer * 8 + 8, 192:224, :] = moved.reshape(8, 32, 128)
            out_ref[16 + layer * 4 : 20 + layer * 4, 192:224, :] = dv[layer].astype(bf16).reshape(4, 32, 128)
        total = jnp.sum(dg[...], axis=1)
        high = total.astype(bf16).astype(f32)
        rest = jnp.concatenate([high, total - high, jnp.zeros((28, 128), f32)], axis=0)
        out_ref[24, 192:224, :] = rest.astype(bf16)
        out_ref[25:32, 192:224, :] = jnp.zeros((7, 32, 128), bf16)


def run_layers(x, out_grad, wcol, wcol_t, expand_w, norm_gain, place):
    bf16, f32 = jnp.bfloat16, jnp.float32
    whole = lambda *shape: pl.BlockSpec(shape, lambda i: (0,) * len(shape))
    return pl.pallas_call(
        layers_kernel,
        grid=(24 // B,),
        out_shape=(
            jax.ShapeDtypeStruct((24, 256, 128), bf16),
            jax.ShapeDtypeStruct((32, 224, 128), bf16),
        ),
        in_specs=[
            pl.BlockSpec((16, B, 16, 128), lambda i: (0, i, 0, 0)),
            pl.BlockSpec((B, 256, 128), lambda i: (i, 0, 0)),
            whole(2, 256, 128),
            whole(2, 128, 256),
            whole(2, 128, 128),
            whole(2, 128),
            whole(256, 256),
        ],
        out_specs=(pl.BlockSpec((B, 256, 128), lambda i: (i, 0, 0)), whole(32, 224, 128)),
        scratch_shapes=[
            pltpu.VMEM((2, 256, 128), f32),
            pltpu.VMEM((2, 128, 128), f32),
            pltpu.VMEM((2, 8, 128), f32),
        ],
        compiler_params=pltpu.CompilerParams(vmem_limit_bytes=40 * 1024 * 1024),
        cost_estimate=pl.CostEstimate(flops=4 * 10**9, bytes_accessed=7 * 2**20, transcendentals=0),
        name="layers",
    )(x, out_grad, wcol, wcol_t, expand_w, norm_gain, place)


def shift_z(x, step):
    return lax.ppermute(x, "z", [(i, (i + step) % 8) for i in range(8)])


def swap_xl(x):
    return lax.ppermute(x, "xl", [(0, 1), (1, 0)])


def on_device(pooled, row_scale, row_ids, feature_order, compress_w, expand_w, norm_gain, out_grad):
    bf16, f32 = jnp.bfloat16, jnp.float32
    xl = lax.axis_index("xl")
    z = lax.axis_index("z")
    place = (feature_order[None, :] == jnp.arange(256, dtype=jnp.int32)[:, None]).astype(bf16)
    wcol = jnp.einsum("fj,lfk->ljk", place, compress_w, preferred_element_type=f32).astype(bf16)
    scaled = (pooled.astype(f32) * row_scale[:, :, None]).astype(bf16)
    wcol_t = jnp.einsum("fj,lfk->lkj", place, compress_w, preferred_element_type=f32).astype(bf16)
    x_zero = lax.all_to_all(scaled, SHARD, split_axis=0, concat_axis=0, tiled=True).reshape(16, 24, 16, 128)

    marks = jnp.stack([row_ids.astype(f32), row_scale]).transpose(0, 2, 1).reshape(2, 2, 8, 384)
    mine = lax.dynamic_index_in_dim(marks, xl, 1, keepdims=False)
    other = swap_xl(lax.dynamic_index_in_dim(marks, 1 - xl, 1, keepdims=False))
    low = xl == 0
    marks = jnp.concatenate([jnp.where(low, mine, other), jnp.where(low, other, mine)], axis=2)

    features_out, parcels = run_layers(x_zero, out_grad, wcol, wcol_t, expand_w, norm_gain, place)
    parcels = lax.all_to_all(parcels, PLANE, split_axis=0, concat_axis=0, tiled=True)

    dense_part = jnp.sum(parcels[:, 192:].astype(f32), axis=0).astype(bf16)
    grads = parcels[:, :192].reshape(768, 8, 128)
    hit = marks[0][:, None, :] == jnp.arange(R, dtype=f32)[None, :, None]
    scale_high = marks[1].astype(bf16)
    scale_low = (marks[1] - scale_high.astype(f32)).astype(bf16)
    none = jnp.zeros((), bf16)
    high = jnp.einsum("frb,bfd->frd", jnp.where(hit, scale_high[:, None, :], none), grads, preferred_element_type=f32)
    low_part = jnp.einsum("frb,bfd->frd", jnp.where(hit, scale_low[:, None, :], none), grads, preferred_element_type=f32)
    table_part = (high + low_part).astype(bf16)
    table_part = jnp.concatenate([table_part, jnp.broadcast_to(dense_part[None], (8, 32, 128))], axis=1)
    table_part = lax.all_to_all(table_part, "z", split_axis=0, concat_axis=0, tiled=True)
    summed = jnp.sum(table_part.astype(f32), axis=0).astype(bf16)
    table, dense_sum = summed[:256], summed[256:]

    copies = jnp.broadcast_to(dense_sum[None], (32, 32, 128))
    other = swap_xl(table)
    copies, other = lax.optimization_barrier((copies, other))
    dense_all = lax.all_to_all(copies, PLANE, split_axis=0, concat_axis=0, tiled=True).reshape(1024, 128)
    pair = jnp.stack([jnp.where(low, table, other), jnp.where(low, other, table)])
    out = jnp.zeros((2, 8, R, 128), f32)

    def put(out, block, owner, start=0):
        return lax.dynamic_update_slice(out, block.astype(f32)[:, None], (0, owner % 8, start, 0))

    out = put(out, pair, z)
    up = down = pair
    for step in range(1, 4):
        up, down = shift_z(up, 1), shift_z(down, -1)
        out = put(out, up, z - step + 8)
        out = put(out, down, z + step)
    up, down, dense_all = lax.optimization_barrier((up, down, dense_all))
    half_up = shift_z(up[:, :128], 1)
    half_down = shift_z(down[:, 128:], -1)
    out = put(out, half_up, z + 4)
    out = put(out, half_down, z + 4, 128)
    table_grad = out.reshape(16, R, 128)
    dense_all = dense_all.astype(f32)
    compress_grad = dense_all[:512].reshape(2, 256, 128)
    expand_grad = dense_all[512:768].reshape(2, 128, 128)
    gain_grad = dense_all[768:770] + dense_all[770:772]

    return (features_out, table_grad, compress_grad, expand_grad, gain_grad)


def solution(mesh):
    split = Mesh(mesh.devices.reshape(8, 2, 4, 2, 2), ("z", "xl", "y", "xh", "core"))
    grp = ("z", "xl")
    return jax.shard_map(
        on_device,
        mesh=split,
        in_specs=(
            P(grp, SHARD, None),
            P(grp, SHARD),
            P(grp, SHARD),
            P(),
            P(),
            P(),
            P(),
            P(grp + SHARD, None, None),
        ),
        out_specs=(P(grp + SHARD, None, None), P(SHARD, None, None), P(), P(), P()),
        check_vma=False,
    )
```
